32 devices in a mesh: groups: 2 (over x), lat: 8 (over z, y), lon: 2 (over core).
Axes of the slice: x: 2, y: 2, z: 4, core: 2. Of those that a mesh axis runs over, the one named last changes fastest.
Arguments:
- grid_lat: bfloat16 [32768, 512], P(('groups', 'lat', 'lon')), parts along dimension 0, may hold values from -6 to 6
- mesh_lat: bfloat16 [8192, 512], P(('groups', 'lat', 'lon')), parts along dimension 0, may hold values from -6 to 6
- edge_lat: bfloat16 [49152, 512], P(('groups', 'lat', 'lon')), parts along dimension 0, may hold values from -6 to 6
- edge_src: int32 [49152], P(('groups', 'lat', 'lon')), parts along dimension 0, may hold values from 0 to 16383, as said below
- edge_dst: int32 [49152], P(('groups', 'lat', 'lon')), parts along dimension 0, may hold values from 0 to 4095, as said below
- edge_mask: int32 [49152], P(('groups', 'lat', 'lon')), parts along dimension 0, may hold values from 0 to 1, as said below
- grid_w1: bfloat16 [512, 512], replicated, may hold values from -0.25 to 0.25
- grid_w2: bfloat16 [512, 512], replicated, may hold values from -0.25 to 0.25
- edge_w_edge: bfloat16 [512, 512], replicated, may hold values from -0.15625 to 0.15625
- edge_w_grid: bfloat16 [512, 512], replicated, may hold values from -0.15625 to 0.15625
- edge_w_mesh: bfloat16 [512, 512], replicated, may hold values from -0.15625 to 0.15625
- edge_w2: bfloat16 [512, 512], replicated, may hold values from -0.25 to 0.25
- mesh_w1: bfloat16 [1024, 512], replicated, may hold values from -0.1875 to 0.1875
- mesh_w2: bfloat16 [512, 512], replicated, may hold values from -0.25 to 0.25
Outputs:
- mesh_out: bfloat16 [8192, 512], P(('groups', 'lat', 'lon')), parts along dimension 0
- grid_out: bfloat16 [32768, 512], P(('groups', 'lat', 'lon')), parts along dimension 0
The draws below stay inside these ranges and needn't reach their ends.
There are 2 independent parts, one for each index of `groups`. The reference program is written for one: setup_inputs(seed, part) draws one part's arguments, and reference() takes and returns one part's arrays. A program takes and returns all parts, laid end to end along the dimension named above; an argument that names none is the same for every part. Nothing has to cross between parts.
Inputs may be any that keep to these rules, and one draw needn't show every extreme that they name: `edge_src`: the edge slots of device d (lat index i, lon index j, d = i * 2 + j) are slots d * 1536 to (d + 1) * 1536 - 1; each takes its source among device d's own grid nodes d * 1024 to (d + 1) * 1024 - 1, and every such grid node is the source of some slot of device d. `edge_dst`: an edge slot of a device with lat index i targets a mesh node of a device with lat index i - 1, i or i + 1 (either lon index). `edge_mask`: on each device the live slots come first, at least 512 of them; on some device all slots are live.
All inputs are finite; a program needn't handle non-finite values.
Results may differ from the reference program's by a relative error of at most 0.0057.
Values may be sent and summed in bfloat16 or wider, within the bound.
A program may use at most 64 MiB of HBM per device.

```python
import jax
import jax.numpy as jnp
from jax import lax

D = 512
GR = 1024
MR = 256
EDGES_DEV = 1536
G = 16384
M = 4096
EDGES = 24576
N_LAT = 8
N_LON = 2


def source_rows(key):
    first, second, third = jax.random.split(key, 3)
    every = jax.random.permutation(first, GR)
    extra = jax.random.randint(second, (EDGES_DEV - GR,), 0, GR)
    return jax.random.permutation(third, jnp.concatenate([every, extra]))


def draw_edge_src(key, part):
    key = jax.random.fold_in(key, 5)
    devices = N_LAT * N_LON
    keys = jax.random.split(key, devices)
    rows = jax.vmap(source_rows)(keys)
    offsets = (jnp.arange(devices, dtype=jnp.int32) * GR)[:, None]
    return (rows.astype(jnp.int32) + offsets).reshape(-1)


def draw_edge_dst(key, part):
    key = jax.random.fold_in(key, 7)
    first, second, third = jax.random.split(key, 3)
    total = EDGES_DEV * N_LAT * N_LON
    device = jnp.arange(total, dtype=jnp.int32) // EDGES_DEV
    band = device // N_LON
    lowest = jnp.where(band == 0, 0, -1)
    highest = jnp.where(band == N_LAT - 1, 1, 2)
    offset = lowest + jax.random.randint(first, (total,), 0, 6) % (highest - lowest)
    column = jax.random.randint(second, (total,), 0, N_LON)
    row_in = jax.random.randint(third, (total,), 0, MR)
    drawn = (((band + offset) * N_LON + column) * MR + row_in).astype(jnp.int32)
    positions = jnp.arange(total, dtype=jnp.int32)
    drawn = jnp.where(positions == 0, 0, drawn)
    drawn = jnp.where(positions == total - 1, MR * N_LAT * N_LON - 1, drawn)
    return drawn.astype(jnp.int32)


def draw_edge_mask(key, part):
    key = jax.random.fold_in(key, 11)
    first, second = jax.random.split(key)
    devices = N_LAT * N_LON
    counts = jax.random.randint(first, (devices,), EDGES_DEV // 3, EDGES_DEV + 1)
    fullest = jax.random.randint(second, (), 0, devices)
    counts = jnp.where(jnp.arange(devices) == fullest, EDGES_DEV, counts)
    slots = jnp.arange(EDGES_DEV, dtype=jnp.int32)
    return (slots[None, :] < counts[:, None]).astype(jnp.int32).reshape(-1)


def levels(stream_key, dims, cuts, low, top_value):
    factor_of, own = 1.0, jax.random.fold_in(stream_key, 6)
    for dim, shards_of in cuts:
        draws = jnp.exp(jax.random.uniform(jax.random.fold_in(own, dim), (shards_of,), jnp.float32, low / len(cuts), top_value / len(cuts)))
        factor_of = factor_of * jnp.repeat(draws, dims[dim] // shards_of).reshape([-1 if axis == dim else 1 for axis in range(len(dims))])
    return factor_of


def gaussian(stream_key, extent, spread, limit, shards=(), kind=jnp.bfloat16):
    values = jax.random.normal(stream_key, extent, jnp.float32) * spread
    if len(shards) > 0:
        values = levels(stream_key, extent, shards, -0.22, 0.18) * values
    return jnp.clip(values, min=-limit, max=limit).astype(kind)


def setup_inputs(seed: int = 0, part: int = 0) -> dict:
    arg_keys = jax.random.split(jax.random.key(seed), 15)
    part_splits = jax.random.split(jax.random.fold_in(arg_keys[14], part), 15)
    grid_lat = gaussian(part_splits[0], (G, D), 1.0, 6.0, ((0, 16),))
    mesh_lat = gaussian(part_splits[1], (M, D), 1.0, 6.0, ((0, 16),))
    edge_lat = gaussian(part_splits[2], (EDGES, D), 1.0, 6.0, ((0, 16),))
    edge_src = draw_edge_src(jax.random.fold_in(jax.random.fold_in(arg_keys[14], part), 71), part)
    edge_dst = draw_edge_dst(jax.random.fold_in(jax.random.fold_in(arg_keys[14], part), 71), part)
    edge_mask = draw_edge_mask(jax.random.fold_in(jax.random.fold_in(arg_keys[14], part), 71), part)
    grid_w1 = gaussian(arg_keys[6], (D, D), D ** -0.5, 0.25)
    grid_w2 = gaussian(arg_keys[7], (D, D), D ** -0.5, 0.25)
    edge_w_edge = gaussian(arg_keys[8], (D, D), (3 * D) ** -0.5, 0.15625)
    edge_w_grid = gaussian(arg_keys[9], (D, D), (3 * D) ** -0.5, 0.15625)
    edge_w_mesh = gaussian(arg_keys[10], (D, D), (3 * D) ** -0.5, 0.15625)
    edge_w2 = gaussian(arg_keys[11], (D, D), D ** -0.5, 0.25)
    mesh_w1 = gaussian(arg_keys[12], (2 * D, D), (2 * D) ** -0.5, 0.1875)
    mesh_w2 = gaussian(arg_keys[13], (D, D), D ** -0.5, 0.25)
    return dict(grid_lat=grid_lat, mesh_lat=mesh_lat, edge_lat=edge_lat, edge_src=edge_src, edge_dst=edge_dst, edge_mask=edge_mask, grid_w1=grid_w1, grid_w2=grid_w2, edge_w_edge=edge_w_edge, edge_w_grid=edge_w_grid, edge_w_mesh=edge_w_mesh, edge_w2=edge_w2, mesh_w1=mesh_w1, mesh_w2=mesh_w2)


def layer_norm(values):
    mean = lax.optimization_barrier(jnp.mean(values, axis=-1, keepdims=True))
    centered = values - mean
    variance = lax.optimization_barrier(jnp.mean(centered * centered, axis=-1, keepdims=True))
    return centered / jnp.sqrt(variance + 1e-05)

def reference(grid_lat, mesh_lat, edge_lat, edge_src, edge_dst, edge_mask, grid_w1, grid_w2, edge_w_edge, edge_w_grid, edge_w_mesh, edge_w2, mesh_w1, mesh_w2):
    grid_mid = jax.nn.silu(jnp.dot(grid_lat, grid_w1, preferred_element_type=jnp.float32)).astype(jnp.bfloat16)
    grid_out = (grid_lat.astype(jnp.float32) + layer_norm(jnp.dot(grid_mid, grid_w2, preferred_element_type=jnp.float32))).astype(jnp.bfloat16)
    grid_part = jnp.dot(grid_lat, edge_w_grid, preferred_element_type=jnp.float32).astype(jnp.bfloat16)
    mesh_part = jnp.dot(mesh_lat, edge_w_mesh, preferred_element_type=jnp.float32).astype(jnp.bfloat16)
    edge_pre = jnp.dot(edge_lat, edge_w_edge, preferred_element_type=jnp.float32)
    edge_pre = edge_pre + jnp.take(grid_part, edge_src, axis=0).astype(jnp.float32)
    edge_pre = edge_pre + jnp.take(mesh_part, edge_dst, axis=0).astype(jnp.float32)
    edge_mid = jax.nn.silu(edge_pre).astype(jnp.bfloat16)
    edge_new = (edge_lat.astype(jnp.float32) + layer_norm(jnp.dot(edge_mid, edge_w2, preferred_element_type=jnp.float32))).astype(jnp.bfloat16)
    weighted = edge_new.astype(jnp.float32) * edge_mask[:, None].astype(jnp.float32)
    agg = jax.ops.segment_sum(weighted, edge_dst, num_segments=mesh_lat.shape[0])
    agg_b = agg.astype(jnp.bfloat16)
    mesh_pre = jnp.dot(mesh_lat, mesh_w1[:D], preferred_element_type=jnp.float32) + jnp.dot(agg_b, mesh_w1[D:], preferred_element_type=jnp.float32)
    mesh_mid = jax.nn.silu(mesh_pre).astype(jnp.bfloat16)
    mesh_out = (mesh_lat.astype(jnp.float32) + layer_norm(jnp.dot(mesh_mid, mesh_w2, preferred_element_type=jnp.float32))).astype(jnp.bfloat16)
    return (mesh_out, grid_out)
```

```python
import functools

import jax
import jax.numpy as jnp
from jax import lax
from jax.experimental import pallas as pl
from jax.experimental.pallas import tpu as pltpu
from jax.sharding import PartitionSpec as P

TILE = 256
CHUNKS = 2
MESH = pl.DeviceIdType.MESH


def silu(v):
    half = 0.5 * v
    return half + half * jnp.tanh(half)


def layer_norm(values):
    mean = jnp.mean(values, axis=-1, keepdims=True)
    centered = values - mean
    variance = jnp.mean(centered * centered, axis=-1, keepdims=True)
    return centered * lax.rsqrt(variance + 1e-05)


def dot(a, b):
    return jnp.dot(a, b, preferred_element_type=jnp.float32)


def spread(ref, tile):
    parts = []
    for k in range(TILE // 128):
        row = ref[pl.ds(tile * (TILE // 128) + k, 1), :]
        parts.append(jnp.broadcast_to(row, (128, 128)).T)
    return jnp.concatenate(parts, axis=0)


def picks(cols, bases, width):
    lanes = lax.broadcasted_iota(jnp.int32, (TILE, 128), 1)
    parts = []
    for base in bases:
        for k in range(width // 128):
            hit = cols == lanes + (base + 128 * k)
            parts.append(jnp.where(hit, 1.0, 0.0).astype(jnp.bfloat16))
    return jnp.concatenate(parts, axis=1)


def rows_of(tile):
    return pl.ds(pl.multiple_of(tile * TILE, TILE), TILE)


def kernel(
    lat_n,
    src_ref,
    dst_ref,
    mask_ref,
    grid_hbm,
    mesh_hbm,
    edge_hbm,
    gw1_hbm,
    gw2_hbm,
    wee_hbm,
    weg_hbm,
    wem_hbm,
    ew2_hbm,
    mw1_hbm,
    mw2_hbm,
    mesh_out,
    grid_out,
    grid,
    mesh,
    edge,
    gw1,
    gw2,
    wee,
    weg,
    wem,
    ew2,
    mw1,
    mw2,
    own,
    halo,
    part,
    pre,
    cols,
    live,
    fresh,
    gout,
    mout,
    pout,
    pin,
    acc,
    send,
    recv,
    mpre,
    in_sem,
    out_sem,
    own_sems,
    halo_send,
    halo_recv,
    fwd_send,
    fwd_recv,
    swap_send,
    swap_recv,
    msg_send,
    msg_recv,
):
    band = lax.axis_index("lat")
    col = lax.axis_index("lon")
    peer = 1 - col
    width = mesh.shape[1]
    mesh_rows = mesh.shape[0]
    grid_rows = grid.shape[0]
    slots_n = edge.shape[0]
    tiles = slots_n // TILE
    piece = mesh_rows // CHUNKS

    order = [
        (mesh_hbm, mesh),
        (wem_hbm, wem),
        (grid_hbm, grid),
        (weg_hbm, weg),
        (edge_hbm, edge),
        (wee_hbm, wee),
        (ew2_hbm, ew2),
        (gw1_hbm, gw1),
        (gw2_hbm, gw2),
        (mw1_hbm, mw1),
        (mw2_hbm, mw2),
    ]
    loads = [
        pltpu.make_async_copy(a, b, in_sem.at[i]) for i, (a, b) in enumerate(order)
    ]
    for load in loads:
        load.start()

    has = [band > 0, band < lat_n - 1]
    toward = [band - 1, band + 1]
    barrier = pltpu.get_barrier_semaphore()
    pl.semaphore_signal(barrier, inc=1, device_id={"lon": peer}, device_id_type=MESH)
    for side in range(2):

        @pl.when(has[side])
        def _():
            pl.semaphore_signal(
                barrier, inc=1, device_id={"lat": toward[side]}, device_id_type=MESH
            )

        @pl.when(jnp.logical_not(has[side]))
        def _():
            for q in range(CHUNKS):
                halo[q, 2 * side] = jnp.zeros((piece, width), jnp.bfloat16)
                halo[q, 2 * side + 1] = jnp.zeros((piece, width), jnp.bfloat16)

    loads[0].wait()
    loads[1].wait()
    own[col] = dot(mesh[...], wem[...]).astype(jnp.bfloat16)

    peers = 1 + jnp.minimum(band, 1) + jnp.minimum(lat_n - 1 - band, 1)
    pl.semaphore_wait(barrier, peers)

    def halo_copy(q, side):
        return pltpu.make_async_remote_copy(
            src_ref=own.at[col, pl.ds(q * piece, piece)],
            dst_ref=halo.at[q, 2 * (1 - side) + col],
            send_sem=halo_send.at[q, side],
            recv_sem=halo_recv.at[q, 1 - side],
            device_id={"lat": toward[side]},
            device_id_type=MESH,
        )

    def halo_arrival(q, side):
        return pltpu.make_async_remote_copy(
            src_ref=own.at[col, pl.ds(q * piece, piece)],
            dst_ref=halo.at[q, 2 * side + col],
            send_sem=halo_send.at[q, side],
            recv_sem=halo_recv.at[q, side],
            device_id={"lat": toward[side]},
            device_id_type=MESH,
        )

    def fwd_copy(q, side):
        return pltpu.make_async_remote_copy(
            src_ref=halo.at[q, 2 * side + col],
            dst_ref=halo.at[q, 2 * side + col],
            send_sem=fwd_send.at[q, side],
            recv_sem=fwd_recv.at[q, side],
            device_id={"lon": peer},
            device_id_type=MESH,
        )

    def fwd_arrival(q, side):
        return pltpu.make_async_remote_copy(
            src_ref=halo.at[q, 2 * side + col],
            dst_ref=halo.at[q, 2 * side + peer],
            send_sem=fwd_send.at[q, side],
            recv_sem=fwd_recv.at[q, side],
            device_id={"lon": peer},
            device_id_type=MESH,
        )

    for q in range(CHUNKS):
        for side in range(2):

            @pl.when(has[side])
            def _():
                halo_copy(q, side).start()

    own_copy = pltpu.make_async_remote_copy(
        src_ref=own.at[col],
        dst_ref=own.at[col],
        send_sem=own_sems.at[0],
        recv_sem=own_sems.at[1],
        device_id={"lon": peer},
        device_id_type=MESH,
    )
    own_copy.start()

    loads[2].wait()
    loads[3].wait()

    def grid_part(t, carry):
        rows = rows_of(t)
        part[rows, :] = dot(grid[rows, :], weg[...]).astype(jnp.bfloat16)
        return carry

    lax.fori_loop(0, grid_rows // TILE, grid_part, 0)

    loads[4].wait()
    loads[5].wait()
    pltpu.make_async_remote_copy(
        src_ref=own.at[col],
        dst_ref=own.at[peer],
        send_sem=own_sems.at[0],
        recv_sem=own_sems.at[1],
        device_id={"lon": peer},
        device_id_type=MESH,
    ).wait_recv()
    first_grid = (band * 2 + col) * grid_rows
    first_mesh = (band - 1) * 2 * mesh_rows
    live[...] = jnp.where(mask_ref[...] == 1, dst_ref[...] - first_mesh, -1)

    def before_halo(t, carry):
        rows = rows_of(t)
        source = spread(src_ref, t)
        target = spread(dst_ref, t) - first_mesh
        cols[rows, :] = target
        total = dot(edge[rows, :], wee[...])
        total += dot(picks(source, [first_grid], grid_rows), part[...])
        total += dot(
            picks(target, [2 * mesh_rows], 2 * mesh_rows),
            own[...].reshape(2 * mesh_rows, width),
        )
        pre[rows, :] = total
        return carry

    lax.fori_loop(0, tiles, before_halo, 0)

    def from_halo(q, target):
        bases = [
            2 * side * 2 * mesh_rows + c * mesh_rows + q * piece
            for side in range(2)
            for c in range(2)
        ]
        return dot(picks(target, bases, piece), halo[q].reshape(4 * piece, width))

    for q in range(CHUNKS):
        for side in range(2):

            @pl.when(has[side])
            def _():
                halo_arrival(q, side).wait_recv()
                fwd_copy(q, side).start()

        for side in range(2):

            @pl.when(has[side])
            def _():
                fwd_arrival(q, side).wait_recv()

        if q < CHUNKS - 1:

            def add_halo(t, carry):
                rows = rows_of(t)
                pre[rows, :] += from_halo(q, cols[rows, :])
                return carry

            lax.fori_loop(0, tiles, add_halo, 0)

    loads[6].wait()

    def edge_mlp(t, carry):
        rows = rows_of(t)
        total = pre[rows, :] + from_halo(CHUNKS - 1, cols[rows, :])
        mid = silu(total).astype(jnp.bfloat16)
        normed = layer_norm(dot(mid, ew2[...]))
        fresh[rows, :] = (edge[rows, :].astype(jnp.float32) + normed).astype(jnp.bfloat16)
        return carry

    lax.fori_loop(0, tiles, edge_mlp, 0)

    def sums(first):
        ids = lax.broadcasted_iota(jnp.int32, (mesh_rows, 128), 0) + first
        parts = []
        for k in range(slots_n // 128):
            hit = jnp.broadcast_to(live[k : k + 1, :], (mesh_rows, 128)) == ids
            parts.append(jnp.where(hit, 1.0, 0.0).astype(jnp.bfloat16))
        return dot(jnp.concatenate(parts, axis=1), fresh[...])

    def swap(i):
        return pltpu.make_async_remote_copy(
            src_ref=pout.at[i],
            dst_ref=pin.at[i],
            send_sem=swap_send.at[i],
            recv_sem=swap_recv.at[i],
            device_id={"lon": peer},
            device_id_type=MESH,
        )

    def message(side):
        return pltpu.make_async_remote_copy(
            src_ref=send.at[side],
            dst_ref=recv.at[side],
            send_sem=msg_send.at[side],
            recv_sem=msg_recv.at[side],
            device_id={"lat": toward[side]},
            device_id_type=MESH,
        )

    def block_first(block, c):
        return (block * 2 + c) * mesh_rows

    for side in range(2):
        pout[side] = sums(block_first(2 * side, peer))
        swap(side).start()
    for side in range(2):
        acc[...] = sums(block_first(2 * side, col))
        swap(side).wait_recv()
        send[side] = (acc[...] + pin[side]).astype(jnp.bfloat16)

        @pl.when(has[side])
        def _():
            message(side).start()

    pout[2] = sums(block_first(1, peer))
    swap(2).start()
    acc[...] = sums(block_first(1, col))

    for i in (7, 8, 9, 10):
        loads[i].wait()

    def grid_mlp(t, carry):
        rows = rows_of(t)
        mid = silu(dot(grid[rows, :], gw1[...])).astype(jnp.bfloat16)
        normed = layer_norm(dot(mid, gw2[...]))
        gout[rows, :] = (grid[rows, :].astype(jnp.float32) + normed).astype(jnp.bfloat16)
        return carry

    lax.fori_loop(0, grid_rows // TILE, grid_mlp, 0)
    store_grid = pltpu.make_async_copy(gout, grid_out, out_sem.at[0])
    store_grid.start()

    mpre[...] = dot(mesh[...], mw1[:width, :])
    swap(2).wait_recv()
    acc[...] += pin[2]
    for side in range(2):

        @pl.when(has[1 - side])
        def _():
            message(side).wait_recv()
            acc[...] += recv[side].astype(jnp.float32)

    mid = silu(mpre[...] + dot(acc[...].astype(jnp.bfloat16), mw1[width:, :])).astype(
        jnp.bfloat16
    )
    normed = layer_norm(dot(mid, mw2[...]))
    mout[...] = (mesh[...].astype(jnp.float32) + normed).astype(jnp.bfloat16)
    store_mesh = pltpu.make_async_copy(mout, mesh_out, out_sem.at[1])
    store_mesh.start()

    own_copy.wait_send()
    for i in range(3):
        swap(i).wait_send()
    for side in range(2):

        @pl.when(has[side])
        def _():
            message(side).wait_send()
            for q in range(CHUNKS):
                halo_copy(q, side).wait_send()
                fwd_copy(q, side).wait_send()

    store_grid.wait()
    store_mesh.wait()


def per_device(lat_n, *args):
    (grid_lat, mesh_lat, edge_lat, edge_src, edge_dst, edge_mask) = args[:6]
    weights = args[6:]
    width = mesh_lat.shape[1]
    mesh_rows = mesh_lat.shape[0]
    grid_rows = grid_lat.shape[0]
    slots = edge_lat.shape[0]
    bf16, f32 = jnp.bfloat16, jnp.float32
    piece = mesh_rows // CHUNKS
    dma = pltpu.SemaphoreType.DMA
    vmem = pltpu.VMEM
    scratch = [
        vmem(grid_lat.shape, bf16),
        vmem(mesh_lat.shape, bf16),
        vmem(edge_lat.shape, bf16),
        *[vmem(w.shape, bf16) for w in weights],
        vmem((2, mesh_rows, width), bf16),
        vmem((CHUNKS, 4, piece, width), bf16),
        vmem((grid_rows, width), bf16),
        vmem((slots, width), f32),
        vmem((slots, 128), jnp.int32),
        vmem((slots // 128, 128), jnp.int32),
        vmem((slots, width), bf16),
        vmem((grid_rows, width), bf16),
        vmem((mesh_rows, width), bf16),
        vmem((3, mesh_rows, width), f32),
        vmem((3, mesh_rows, width), f32),
        vmem((mesh_rows, width), f32),
        vmem((2, mesh_rows, width), bf16),
        vmem((2, mesh_rows, width), bf16),
        vmem((mesh_rows, width), f32),
        dma((11,)),
        dma((2,)),
        dma((2,)),
        dma((CHUNKS, 2)),
        dma((CHUNKS, 2)),
        dma((CHUNKS, 2)),
        dma((CHUNKS, 2)),
        dma((3,)),
        dma((3,)),
        dma((2,)),
        dma((2,)),
    ]
    in_vmem = pl.BlockSpec(memory_space=pltpu.VMEM)
    anywhere = pl.BlockSpec(memory_space=pl.ANY)
    return pl.pallas_call(
        functools.partial(kernel, lat_n),
        out_shape=(
            jax.ShapeDtypeStruct(mesh_lat.shape, bf16),
            jax.ShapeDtypeStruct(grid_lat.shape, bf16),
        ),
        in_specs=[in_vmem] * 3 + [anywhere] * 11,
        out_specs=(anywhere, anywhere),
        scratch_shapes=scratch,
        compiler_params=pltpu.CompilerParams(
            collective_id=0, has_side_effects=True, vmem_limit_bytes=48 * 2**20
        ),
    )(
        *[a.reshape(slots // 128, 128) for a in (edge_src, edge_dst, edge_mask)],
        grid_lat,
        mesh_lat,
        edge_lat,
        *weights,
    )


def solution(mesh):
    rows = P(("groups", "lat", "lon"), None)
    line = P(("groups", "lat", "lon"))
    return jax.shard_map(
        functools.partial(per_device, mesh.shape["lat"]),
        mesh=mesh,
        in_specs=(rows,) * 3 + (line,) * 3 + (P(),) * 8,
        out_specs=(rows, rows),
        check_vma=False,
    )
```

```python
import functools

import jax
import jax.numpy as jnp
from jax import lax
from jax.experimental import pallas as pl
from jax.experimental.pallas import tpu as pltpu
from jax.sharding import PartitionSpec as P

TILE = 256
CHUNKS = 2
VMEM_BYTES = 63 * 2**20
MESH = pl.DeviceIdType.MESH


def silu(v):
    half = 0.5 * v
    return half + half * jnp.tanh(half)


def layer_norm(values):
    mean = jnp.mean(values, axis=-1, keepdims=True)
    centered = values - mean
    variance = jnp.mean(centered * centered, axis=-1, keepdims=True)
    return centered * lax.rsqrt(variance + 1e-05)


def dot(a, b):
    return jnp.dot(a, b, preferred_element_type=jnp.float32)


def spread(ref, tile):
    parts = []
    for k in range(TILE // 128):
        row = ref[pl.ds(tile * (TILE // 128) + k, 1), :]
        parts.append(jnp.broadcast_to(row, (128, 128)).T)
    return jnp.concatenate(parts, axis=0)


def picks(cols, bases, width):
    lanes = lax.broadcasted_iota(jnp.int32, (TILE, 128), 1)
    parts = []
    for base in bases:
        for k in range(width // 128):
            hit = cols == lanes + (base + 128 * k)
            parts.append(jnp.where(hit, 1.0, 0.0).astype(jnp.bfloat16))
    return jnp.concatenate(parts, axis=1)


def rows_of(tile):
    return pl.ds(pl.multiple_of(tile * TILE, TILE), TILE)


def kernel(
    lat_n,
    src_ref,
    dst_ref,
    mask_ref,
    grid_hbm,
    mesh_hbm,
    edge_hbm,
    gw1_hbm,
    gw2_hbm,
    wee_hbm,
    weg_hbm,
    wem_hbm,
    ew2_hbm,
    mw1_hbm,
    mw2_hbm,
    mesh_out,
    grid_out,
    grid,
    mesh,
    edge,
    gw1,
    gw2,
    wee,
    weg,
    wem,
    ew2,
    mw1,
    mw2,
    own,
    halo,
    part,
    pre,
    cols,
    live,
    fresh,
    gout,
    mout,
    pout,
    pin,
    acc,
    send,
    recv,
    mpre,
    in_sem,
    out_sem,
    own_sems,
    halo_send,
    halo_recv,
    fwd_send,
    fwd_recv,
    swap_send,
    swap_recv,
    msg_send,
    msg_recv,
):
    band = lax.axis_index("lat")
    col = lax.axis_index("lon")
    peer = 1 - col
    width = mesh.shape[1]
    mesh_rows = mesh.shape[0]
    grid_rows = grid.shape[0]
    slots_n = edge.shape[0]
    tiles = slots_n // TILE
    piece = mesh_rows // CHUNKS

    order = [
        (mesh_hbm, mesh),
        (wem_hbm, wem),
        (grid_hbm, grid),
        (weg_hbm, weg),
        (edge_hbm, edge),
        (wee_hbm, wee),
        (ew2_hbm, ew2),
        (gw1_hbm, gw1),
        (gw2_hbm, gw2),
        (mw1_hbm, mw1),
        (mw2_hbm, mw2),
    ]
    loads = [
        pltpu.make_async_copy(a, b, in_sem.at[i]) for i, (a, b) in enumerate(order)
    ]
    for load in loads[:2]:
        load.start()

    has = [band > 0, band < lat_n - 1]
    toward = [band - 1, band + 1]
    barrier = pltpu.get_barrier_semaphore()
    pl.semaphore_signal(barrier, inc=1, device_id={"lon": peer}, device_id_type=MESH)
    for side in range(2):

        @pl.when(has[side])
        def _():
            pl.semaphore_signal(
                barrier, inc=1, device_id={"lat": toward[side]}, device_id_type=MESH
            )

        @pl.when(jnp.logical_not(has[side]))
        def _():
            halo[side] = jnp.zeros((2, mesh_rows, width), jnp.bfloat16)

    loads[0].wait()
    loads[1].wait()
    for load in loads[2:]:
        load.start()
    own[col] = dot(mesh[...], wem[...]).astype(jnp.bfloat16)

    peers = 1 + jnp.minimum(band, 1) + jnp.minimum(lat_n - 1 - band, 1)
    pl.semaphore_wait(barrier, peers)

    def halo_copy(q, side):
        return pltpu.make_async_remote_copy(
            src_ref=own.at[col, pl.ds(q * piece, piece)],
            dst_ref=halo.at[1 - side, col, pl.ds(q * piece, piece)],
            send_sem=halo_send.at[q, side],
            recv_sem=halo_recv.at[q, 1 - side],
            device_id={"lat": toward[side]},
            device_id_type=MESH,
        )

    def halo_arrival(q, side):
        return pltpu.make_async_remote_copy(
            src_ref=own.at[col, pl.ds(q * piece, piece)],
            dst_ref=halo.at[side, col, pl.ds(q * piece, piece)],
            send_sem=halo_send.at[q, side],
            recv_sem=halo_recv.at[q, side],
            device_id={"lat": toward[side]},
            device_id_type=MESH,
        )

    def fwd_copy(q, side):
        return pltpu.make_async_remote_copy(
            src_ref=halo.at[side, col, pl.ds(q * piece, piece)],
            dst_ref=halo.at[side, col, pl.ds(q * piece, piece)],
            send_sem=fwd_send.at[q, side],
            recv_sem=fwd_recv.at[q, side],
            device_id={"lon": peer},
            device_id_type=MESH,
        )

    def fwd_arrival(q, side):
        return pltpu.make_async_remote_copy(
            src_ref=halo.at[side, col, pl.ds(q * piece, piece)],
            dst_ref=halo.at[side, peer, pl.ds(q * piece, piece)],
            send_sem=fwd_send.at[q, side],
            recv_sem=fwd_recv.at[q, side],
            device_id={"lon": peer},
            device_id_type=MESH,
        )

    def send_halo(side):
        @pl.when(has[side])
        def _():
            for q in range(CHUNKS):
                halo_copy(q, side).start()

    send_halo(1)
    own_copy = pltpu.make_async_remote_copy(
        src_ref=own.at[col],
        dst_ref=own.at[col],
        send_sem=own_sems.at[0],
        recv_sem=own_sems.at[1],
        device_id={"lon": peer},
        device_id_type=MESH,
    )
    own_copy.start()

    loads[2].wait()
    loads[3].wait()

    def grid_part(t, carry):
        rows = rows_of(t)
        part[rows, :] = dot(grid[rows, :], weg[...]).astype(jnp.bfloat16)
        return carry

    lax.fori_loop(0, grid_rows // TILE, grid_part, 0)

    loads[4].wait()
    loads[5].wait()
    pltpu.make_async_remote_copy(
        src_ref=own.at[col],
        dst_ref=own.at[peer],
        send_sem=own_sems.at[0],
        recv_sem=own_sems.at[1],
        device_id={"lon": peer},
        device_id_type=MESH,
    ).wait_recv()
    first_grid = (band * 2 + col) * grid_rows
    first_mesh = (band - 1) * 2 * mesh_rows
    live[...] = jnp.where(mask_ref[...] == 1, dst_ref[...] - first_mesh, -1)

    def before_halo(t, carry):
        rows = rows_of(t)
        source = spread(src_ref, t)
        target = spread(dst_ref, t) - first_mesh
        cols[rows, :] = target
        total = dot(edge[rows, :], wee[...])
        total += dot(picks(source, [first_grid], grid_rows), part[...])
        total += dot(
            picks(target, [2 * mesh_rows], 2 * mesh_rows),
            own[...].reshape(2 * mesh_rows, width),
        )
        pre[rows, :] = total
        return carry

    lax.fori_loop(0, tiles, before_halo, 0)

    send_halo(0)
    loads[6].wait()

    def receive_halo(side):
        @pl.when(has[side])
        def _():
            for q in range(CHUNKS):
                halo_arrival(q, side).wait_recv()
                fwd_copy(q, side).start()
            for q in range(CHUNKS):
                fwd_arrival(q, side).wait_recv()

    def edge_mlp(side):
        def step(t, carry):
            for k in range(2):
                rows = rows_of(2 * t + k)
                hits = picks(cols[rows, :], [4 * side * mesh_rows], 2 * mesh_rows)
                total = pre[rows, :] + dot(hits, halo[side].reshape(2 * mesh_rows, width))
                mid = silu(total).astype(jnp.bfloat16)
                normed = layer_norm(dot(mid, ew2[...]))
                fresh[rows, :] = (edge[rows, :].astype(jnp.float32) + normed).astype(
                    jnp.bfloat16
                )
            return carry

        lax.fori_loop(0, tiles // 2, step, 0)

    def sums(first):
        ids = lax.broadcasted_iota(jnp.int32, (mesh_rows, 128), 0) + first
        parts = []
        for k in range(slots_n // 128):
            hit = jnp.broadcast_to(live[k : k + 1, :], (mesh_rows, 128)) == ids
            parts.append(jnp.where(hit, 1.0, 0.0).astype(jnp.bfloat16))
        return dot(jnp.concatenate(parts, axis=1), fresh[...])

    def swap(i):
        return pltpu.make_async_remote_copy(
            src_ref=pout.at[i],
            dst_ref=pin.at[i],
            send_sem=swap_send.at[i],
            recv_sem=swap_recv.at[i],
            device_id={"lon": peer},
            device_id_type=MESH,
        )

    def message(side):
        return pltpu.make_async_remote_copy(
            src_ref=send.at[side],
            dst_ref=recv.at[side],
            send_sem=msg_send.at[side],
            recv_sem=msg_recv.at[side],
            device_id={"lat": toward[side]},
            device_id_type=MESH,
        )

    def block_first(block, c):
        return (block * 2 + c) * mesh_rows

    for side in range(2):
        receive_halo(side)
        edge_mlp(side)
        pout[side] = sums(block_first(2 * side, peer))
        swap(side).start()
        acc[...] = sums(block_first(2 * side, col))
        swap(side).wait_recv()
        send[side] = (acc[...] + pin[side]).astype(jnp.bfloat16)

        @pl.when(has[side])
        def _():
            message(side).start()

    pout[2] = sums(block_first(1, peer))
    swap(2).start()
    acc[...] = sums(block_first(1, col))

    for i in (7, 8, 9, 10):
        loads[i].wait()

    def grid_mlp(t, carry):
        rows = rows_of(t)
        mid = silu(dot(grid[rows, :], gw1[...])).astype(jnp.bfloat16)
        normed = layer_norm(dot(mid, gw2[...]))
        gout[rows, :] = (grid[rows, :].astype(jnp.float32) + normed).astype(jnp.bfloat16)
        return carry

    lax.fori_loop(0, grid_rows // TILE, grid_mlp, 0)
    store_grid = pltpu.make_async_copy(gout, grid_out, out_sem.at[0])
    store_grid.start()

    mpre[...] = dot(mesh[...], mw1[:width, :])
    swap(2).wait_recv()
    acc[...] += pin[2]
    for side in range(2):

        @pl.when(has[1 - side])
        def _():
            message(side).wait_recv()
            acc[...] += recv[side].astype(jnp.float32)

    mid = silu(mpre[...] + dot(acc[...].astype(jnp.bfloat16), mw1[width:, :])).astype(
        jnp.bfloat16
    )
    normed = layer_norm(dot(mid, mw2[...]))
    mout[...] = (mesh[...].astype(jnp.float32) + normed).astype(jnp.bfloat16)
    store_mesh = pltpu.make_async_copy(mout, mesh_out, out_sem.at[1])
    store_mesh.start()

    own_copy.wait_send()
    for i in range(3):
        swap(i).wait_send()
    for side in range(2):

        @pl.when(has[side])
        def _():
            message(side).wait_send()
            for q in range(CHUNKS):
                halo_copy(q, side).wait_send()
                fwd_copy(q, side).wait_send()

    store_grid.wait()
    store_mesh.wait()


def per_device(lat_n, *args):
    (grid_lat, mesh_lat, edge_lat, edge_src, edge_dst, edge_mask) = args[:6]
    weights = args[6:]
    width = mesh_lat.shape[1]
    mesh_rows = mesh_lat.shape[0]
    grid_rows = grid_lat.shape[0]
    slots = edge_lat.shape[0]
    bf16, f32 = jnp.bfloat16, jnp.float32
    dma = pltpu.SemaphoreType.DMA
    vmem = pltpu.VMEM
    scratch = [
        vmem(grid_lat.shape, bf16),
        vmem(mesh_lat.shape, bf16),
        vmem(edge_lat.shape, bf16),
        *[vmem(w.shape, bf16) for w in weights],
        vmem((2, mesh_rows, width), bf16),
        vmem((2, 2, mesh_rows, width), bf16),
        vmem((grid_rows, width), bf16),
        vmem((slots, width), f32),
        vmem((slots, 128), jnp.int32),
        vmem((slots // 128, 128), jnp.int32),
        vmem((slots, width), bf16),
        vmem((grid_rows, width), bf16),
        vmem((mesh_rows, width), bf16),
        vmem((3, mesh_rows, width), f32),
        vmem((3, mesh_rows, width), f32),
        vmem((mesh_rows, width), f32),
        vmem((2, mesh_rows, width), bf16),
        vmem((2, mesh_rows, width), bf16),
        vmem((mesh_rows, width), f32),
        dma((11,)),
        dma((2,)),
        dma((2,)),
        dma((CHUNKS, 2)),
        dma((CHUNKS, 2)),
        dma((CHUNKS, 2)),
        dma((CHUNKS, 2)),
        dma((3,)),
        dma((3,)),
        dma((2,)),
        dma((2,)),
    ]
    in_vmem = pl.BlockSpec(memory_space=pltpu.VMEM)
    anywhere = pl.BlockSpec(memory_space=pl.ANY)
    return pl.pallas_call(
        functools.partial(kernel, lat_n),
        out_shape=(
            jax.ShapeDtypeStruct(mesh_lat.shape, bf16),
            jax.ShapeDtypeStruct(grid_lat.shape, bf16),
        ),
        in_specs=[in_vmem] * 3 + [anywhere] * 11,
        out_specs=(anywhere, anywhere),
        scratch_shapes=scratch,
        compiler_params=pltpu.CompilerParams(
            collective_id=0, has_side_effects=True, vmem_limit_bytes=VMEM_BYTES
        ),
    )(
        *[a.reshape(slots // 128, 128) for a in (edge_src, edge_dst, edge_mask)],
        grid_lat,
        mesh_lat,
        edge_lat,
        *weights,
    )


def solution(mesh):
    rows = P(("groups", "lat", "lon"), None)
    line = P(("groups", "lat", "lon"))
    return jax.shard_map(
        functools.partial(per_device, mesh.shape["lat"]),
        mesh=mesh,
        in_specs=(rows,) * 3 + (line,) * 3 + (P(),) * 8,
        out_specs=(rows, rows),
        check_vma=False,
    )
```

```python
import functools

import jax
import jax.numpy as jnp
from jax import lax
from jax.experimental import pallas as pl
from jax.experimental.pallas import tpu as pltpu
from jax.sharding import PartitionSpec as P

TILE = 256
CHUNKS = 4
EARLY = 2
PARTS = 2
VMEM_BYTES = 63 * 2**20
MESH = pl.DeviceIdType.MESH


def silu(v):
    half = 0.5 * v
    return half + half * jnp.tanh(half)


def layer_norm(values):
    mean = jnp.mean(values, axis=-1, keepdims=True)
    centered = values - mean
    variance = jnp.mean(centered * centered, axis=-1, keepdims=True)
    return centered * lax.rsqrt(variance + 1e-05)


def dot(a, b):
    return jnp.dot(a, b, preferred_element_type=jnp.float32)


def spread(ref, tile):
    parts = []
    for k in range(TILE // 128):
        row = ref[pl.ds(tile * (TILE // 128) + k, 1), :]
        parts.append(jnp.broadcast_to(row, (128, 128)).T)
    return jnp.concatenate(parts, axis=0)


def picks(cols, bases, width):
    lanes = lax.broadcasted_iota(jnp.int32, (TILE, 128), 1)
    parts = []
    for base in bases:
        for k in range(width // 128):
            hit = cols == lanes + (base + 128 * k)
            parts.append(jnp.where(hit, 1.0, 0.0).astype(jnp.bfloat16))
    return jnp.concatenate(parts, axis=1)


def rows_of(tile):
    return pl.ds(pl.multiple_of(tile * TILE, TILE), TILE)


def kernel(
    lat_n,
    src_ref,
    dst_ref,
    mask_ref,
    grid_hbm,
    mesh_hbm,
    edge_hbm,
    gw1_hbm,
    gw2_hbm,
    wee_hbm,
    weg_hbm,
    wem_hbm,
    ew2_hbm,
    mw1_hbm,
    mw2_hbm,
    mesh_out,
    grid_out,
    grid,
    mesh,
    edge,
    gw1,
    gw2,
    wee,
    weg,
    wem,
    ew2,
    mw1,
    mw2,
    own,
    halo,
    part,
    pre,
    cols,
    live,
    fresh,
    gout,
    mout,
    pout,
    pin,
    acc,
    send,
    recv,
    mpre,
    in_sem,
    out_sem,
    own_sems,
    halo_send,
    halo_recv,
    fwd_send,
    fwd_recv,
    swap_send,
    swap_recv,
    msg_send,
    msg_recv,
):
    band = lax.axis_index("lat")
    col = lax.axis_index("lon")
    peer = 1 - col
    width = mesh.shape[1]
    mesh_rows = mesh.shape[0]
    grid_rows = grid.shape[0]
    slots_n = edge.shape[0]
    tiles = slots_n // TILE
    piece = mesh_rows // CHUNKS

    order = [
        (mesh_hbm, mesh),
        (wem_hbm, wem),
        (grid_hbm, grid),
        (weg_hbm, weg),
        (edge_hbm, edge),
        (wee_hbm, wee),
        (ew2_hbm, ew2),
        (gw1_hbm, gw1),
        (gw2_hbm, gw2),
        (mw1_hbm, mw1),
        (mw2_hbm, mw2),
    ]
    loads = [
        pltpu.make_async_copy(a, b, in_sem.at[i]) for i, (a, b) in enumerate(order)
    ]
    for load in loads[:2]:
        load.start()

    has = [band > 0, band < lat_n - 1]
    toward = [band - 1, band + 1]
    barrier = pltpu.get_barrier_semaphore()
    pl.semaphore_signal(barrier, inc=1, device_id={"lon": peer}, device_id_type=MESH)
    for side in range(2):

        @pl.when(has[side])
        def _():
            pl.semaphore_signal(
                barrier, inc=1, device_id={"lat": toward[side]}, device_id_type=MESH
            )

        @pl.when(jnp.logical_not(has[side]))
        def _():
            halo[side] = jnp.zeros((2, mesh_rows, width), jnp.bfloat16)

    loads[0].wait()
    loads[1].wait()
    for load in loads[2:]:
        load.start()
    own[col] = dot(mesh[...], wem[...]).astype(jnp.bfloat16)

    peers = 1 + jnp.minimum(band, 1) + jnp.minimum(lat_n - 1 - band, 1)
    pl.semaphore_wait(barrier, peers)

    def halo_copy(q, side):
        return pltpu.make_async_remote_copy(
            src_ref=own.at[col, pl.ds(q * piece, piece)],
            dst_ref=halo.at[1 - side, col, pl.ds(q * piece, piece)],
            send_sem=halo_send.at[q, side],
            recv_sem=halo_recv.at[q, 1 - side],
            device_id={"lat": toward[side]},
            device_id_type=MESH,
        )

    def halo_arrival(q, side):
        return pltpu.make_async_remote_copy(
            src_ref=own.at[col, pl.ds(q * piece, piece)],
            dst_ref=halo.at[side, col, pl.ds(q * piece, piece)],
            send_sem=halo_send.at[q, side],
            recv_sem=halo_recv.at[q, side],
            device_id={"lat": toward[side]},
            device_id_type=MESH,
        )

    def fwd_copy(q, side):
        return pltpu.make_async_remote_copy(
            src_ref=halo.at[side, col, pl.ds(q * piece, piece)],
            dst_ref=halo.at[side, col, pl.ds(q * piece, piece)],
            send_sem=fwd_send.at[q, side],
            recv_sem=fwd_recv.at[q, side],
            device_id={"lon": peer},
            device_id_type=MESH,
        )

    def fwd_arrival(q, side):
        return pltpu.make_async_remote_copy(
            src_ref=halo.at[side, col, pl.ds(q * piece, piece)],
            dst_ref=halo.at[side, peer, pl.ds(q * piece, piece)],
            send_sem=fwd_send.at[q, side],
            recv_sem=fwd_recv.at[q, side],
            device_id={"lon": peer},
            device_id_type=MESH,
        )

    def send_halo(side):
        @pl.when(has[side])
        def _():
            for q in range(CHUNKS):
                halo_copy(q, side).start()

    send_halo(1)
    own_copy = pltpu.make_async_remote_copy(
        src_ref=own.at[col],
        dst_ref=own.at[col],
        send_sem=own_sems.at[0],
        recv_sem=own_sems.at[1],
        device_id={"lon": peer},
        device_id_type=MESH,
    )
    own_copy.start()

    loads[2].wait()
    loads[3].wait()

    def grid_part(t, carry):
        rows = rows_of(t)
        part[rows, :] = dot(grid[rows, :], weg[...]).astype(jnp.bfloat16)
        return carry

    lax.fori_loop(0, grid_rows // TILE, grid_part, 0)

    loads[4].wait()
    loads[5].wait()
    pltpu.make_async_remote_copy(
        src_ref=own.at[col],
        dst_ref=own.at[peer],
        send_sem=own_sems.at[0],
        recv_sem=own_sems.at[1],
        device_id={"lon": peer},
        device_id_type=MESH,
    ).wait_recv()
    first_grid = (band * 2 + col) * grid_rows
    first_mesh = (band - 1) * 2 * mesh_rows
    live[...] = jnp.where(mask_ref[...] == 1, dst_ref[...] - first_mesh, -1)

    def before_halo(pair, carry):
        for t in (2 * pair, 2 * pair + 1):
            rows = rows_of(t)
            source = spread(src_ref, t)
            target = spread(dst_ref, t) - first_mesh
            cols[rows, :] = target
            total = dot(edge[rows, :], wee[...])
            total += dot(picks(source, [first_grid], grid_rows), part[...])
            total += dot(
                picks(target, [2 * mesh_rows], 2 * mesh_rows),
                own[...].reshape(2 * mesh_rows, width),
            )
            pre[rows, :] = total
        return carry

    lax.fori_loop(0, tiles // 2, before_halo, 0)

    send_halo(0)
    loads[6].wait()

    def forward_halo(side, chunks):
        @pl.when(has[side])
        def _():
            for q in chunks:
                halo_arrival(q, side).wait_recv()
                fwd_copy(q, side).start()

    def receive_halo(side):
        @pl.when(has[side])
        def _():
            for q in range(CHUNKS):
                fwd_arrival(q, side).wait_recv()

    def edge_mlp(side):
        def step(t, carry):
            for k in range(2):
                rows = rows_of(2 * t + k)
                hits = picks(cols[rows, :], [4 * side * mesh_rows], 2 * mesh_rows)
                total = pre[rows, :] + dot(hits, halo[side].reshape(2 * mesh_rows, width))
                mid = silu(total).astype(jnp.bfloat16)
                normed = layer_norm(dot(mid, ew2[...]))
                fresh[rows, :] = (edge[rows, :].astype(jnp.float32) + normed).astype(
                    jnp.bfloat16
                )
            return carry

        lax.fori_loop(0, tiles // 2, step, 0)

    def sums(first):
        ids = lax.broadcasted_iota(jnp.int32, (mesh_rows, 128), 0) + first
        parts = []
        for k in range(slots_n // 128):
            hit = jnp.broadcast_to(live[k : k + 1, :], (mesh_rows, 128)) == ids
            parts.append(jnp.where(hit, 1.0, 0.0).astype(jnp.bfloat16))
        return dot(jnp.concatenate(parts, axis=1), fresh[...])

    def swap(i):
        return pltpu.make_async_remote_copy(
            src_ref=pout.at[i],
            dst_ref=pin.at[i],
            send_sem=swap_send.at[i],
            recv_sem=swap_recv.at[i],
            device_id={"lon": peer},
            device_id_type=MESH,
        )

    some = mesh_rows // PARTS

    def message(side, h):
        return pltpu.make_async_remote_copy(
            src_ref=send.at[side, pl.ds(h * some, some)],
            dst_ref=recv.at[side, pl.ds(h * some, some)],
            send_sem=msg_send.at[side, h],
            recv_sem=msg_recv.at[side, h],
            device_id={"lat": toward[side]},
            device_id_type=MESH,
        )

    def block_first(block, c):
        return (block * 2 + c) * mesh_rows

    def send_message(side):
        @pl.when(has[side])
        def _():
            for h in range(PARTS):
                message(side, h).start()

    forward_halo(0, range(CHUNKS))
    receive_halo(0)
    edge_mlp(0)
    forward_halo(1, range(EARLY))
    pout[0] = sums(block_first(0, peer))
    swap(0).start()
    acc[...] = sums(block_first(0, col))
    swap(0).wait_recv()
    send[0] = (acc[...] + pin[0]).astype(jnp.bfloat16)
    send_message(0)

    forward_halo(1, range(EARLY, CHUNKS))
    pout[2] = sums(block_first(1, peer))
    swap(2).start()
    acc[...] = sums(block_first(1, col))
    receive_halo(1)
    edge_mlp(1)
    pout[1] = sums(block_first(2, peer))
    swap(1).start()
    mpre[...] = sums(block_first(2, col))
    swap(1).wait_recv()
    send[1] = (mpre[...] + pin[1]).astype(jnp.bfloat16)
    send_message(1)

    for i in (7, 8, 9, 10):
        loads[i].wait()

    def grid_mlp(t, carry):
        rows = rows_of(t)
        mid = silu(dot(grid[rows, :], gw1[...])).astype(jnp.bfloat16)
        normed = layer_norm(dot(mid, gw2[...]))
        gout[rows, :] = (grid[rows, :].astype(jnp.float32) + normed).astype(jnp.bfloat16)
        return carry

    lax.fori_loop(0, grid_rows // TILE, grid_mlp, 0)
    store_grid = pltpu.make_async_copy(gout, grid_out, out_sem.at[0])
    store_grid.start()

    mpre[...] = dot(mesh[...], mw1[:width, :])
    swap(2).wait_recv()
    acc[...] += pin[2]
    stores = []
    for h in range(PARTS):
        rows = pl.ds(h * some, some)
        for side in range(2):

            @pl.when(has[1 - side])
            def _():
                message(side, h).wait_recv()
                acc[rows, :] += recv[side, rows, :].astype(jnp.float32)

        mid = silu(
            mpre[rows, :] + dot(acc[rows, :].astype(jnp.bfloat16), mw1[width:, :])
        ).astype(jnp.bfloat16)
        normed = layer_norm(dot(mid, mw2[...]))
        mout[rows, :] = (mesh[rows, :].astype(jnp.float32) + normed).astype(jnp.bfloat16)
        store = pltpu.make_async_copy(
            mout.at[rows], mesh_out.at[rows], out_sem.at[1 + h]
        )
        store.start()
        stores.append(store)

    own_copy.wait_send()
    for i in range(3):
        swap(i).wait_send()
    for side in range(2):

        @pl.when(has[side])
        def _():
            for h in range(PARTS):
                message(side, h).wait_send()
            for q in range(CHUNKS):
                halo_copy(q, side).wait_send()
                fwd_copy(q, side).wait_send()

    store_grid.wait()
    for store in stores:
        store.wait()


def per_device(lat_n, *args):
    (grid_lat, mesh_lat, edge_lat, edge_src, edge_dst, edge_mask) = args[:6]
    weights = args[6:]
    width = mesh_lat.shape[1]
    mesh_rows = mesh_lat.shape[0]
    grid_rows = grid_lat.shape[0]
    slots = edge_lat.shape[0]
    bf16, f32 = jnp.bfloat16, jnp.float32
    dma = pltpu.SemaphoreType.DMA
    vmem = pltpu.VMEM
    scratch = [
        vmem(grid_lat.shape, bf16),
        vmem(mesh_lat.shape, bf16),
        vmem(edge_lat.shape, bf16),
        *[vmem(w.shape, bf16) for w in weights],
        vmem((2, mesh_rows, width), bf16),
        vmem((2, 2, mesh_rows, width), bf16),
        vmem((grid_rows, width), bf16),
        vmem((slots, width), f32),
        vmem((slots, 128), jnp.int32),
        vmem((slots // 128, 128), jnp.int32),
        vmem((slots, width), bf16),
        vmem((grid_rows, width), bf16),
        vmem((mesh_rows, width), bf16),
        vmem((3, mesh_rows, width), f32),
        vmem((3, mesh_rows, width), f32),
        vmem((mesh_rows, width), f32),
        vmem((2, mesh_rows, width), bf16),
        vmem((2, mesh_rows, width), bf16),
        vmem((mesh_rows, width), f32),
        dma((11,)),
        dma((1 + PARTS,)),
        dma((2,)),
        dma((CHUNKS, 2)),
        dma((CHUNKS, 2)),
        dma((CHUNKS, 2)),
        dma((CHUNKS, 2)),
        dma((3,)),
        dma((3,)),
        dma((2, PARTS)),
        dma((2, PARTS)),
    ]
    in_vmem = pl.BlockSpec(memory_space=pltpu.VMEM)
    anywhere = pl.BlockSpec(memory_space=pl.ANY)
    return pl.pallas_call(
        functools.partial(kernel, lat_n),
        out_shape=(
            jax.ShapeDtypeStruct(mesh_lat.shape, bf16),
            jax.ShapeDtypeStruct(grid_lat.shape, bf16),
        ),
        in_specs=[in_vmem] * 3 + [anywhere] * 11,
        out_specs=(anywhere, anywhere),
        scratch_shapes=scratch,
        compiler_params=pltpu.CompilerParams(
            collective_id=0, has_side_effects=True, vmem_limit_bytes=VMEM_BYTES
        ),
    )(
        *[a.reshape(slots // 128, 128) for a in (edge_src, edge_dst, edge_mask)],
        grid_lat,
        mesh_lat,
        edge_lat,
        *weights,
    )


def solution(mesh):
    rows = P(("groups", "lat", "lon"), None)
    line = P(("groups", "lat", "lon"))
    return jax.shard_map(
        functools.partial(per_device, mesh.shape["lat"]),
        mesh=mesh,
        in_specs=(rows,) * 3 + (line,) * 3 + (P(),) * 8,
        out_specs=(rows, rows),
        check_vma=False,
    )
```

```python
import functools

import jax
import jax.numpy as jnp
from jax import lax
from jax.experimental import pallas as pl
from jax.experimental.pallas import tpu as pltpu
from jax.sharding import PartitionSpec as P

TILE = 256
CHUNKS = 2
EARLY = 0
PARTS = 1
VMEM_BYTES = 63 * 2**20
MESH = pl.DeviceIdType.MESH


def silu(v):
    half = 0.5 * v
    return half + half * jnp.tanh(half)


def layer_norm(values):
    mean = jnp.mean(values, axis=-1, keepdims=True)
    centered = values - mean
    variance = jnp.mean(centered * centered, axis=-1, keepdims=True)
    return centered * lax.rsqrt(variance + 1e-05)


def dot(a, b):
    return jnp.dot(a, b, preferred_element_type=jnp.float32)


def spread(ref, tile):
    parts = []
    for k in range(TILE // 128):
        row = ref[pl.ds(tile * (TILE // 128) + k, 1), :]
        parts.append(jnp.broadcast_to(row, (128, 128)).T)
    return jnp.concatenate(parts, axis=0)


def picks(cols, bases, width):
    lanes = lax.broadcasted_iota(jnp.int32, (TILE, 128), 1)
    parts = []
    for base in bases:
        for k in range(width // 128):
            hit = cols == lanes + (base + 128 * k)
            parts.append(jnp.where(hit, 1.0, 0.0).astype(jnp.bfloat16))
    return jnp.concatenate(parts, axis=1)


def rows_of(tile):
    return pl.ds(pl.multiple_of(tile * TILE, TILE), TILE)


def kernel(
    lat_n,
    src_ref,
    dst_ref,
    mask_ref,
    grid_hbm,
    mesh_hbm,
    edge_hbm,
    gw1_hbm,
    gw2_hbm,
    wee_hbm,
    weg_hbm,
    wem_hbm,
    ew2_hbm,
    mw1_hbm,
    mw2_hbm,
    mesh_out,
    grid_out,
    grid,
    mesh,
    edge,
    gw1,
    gw2,
    wee,
    weg,
    wem,
    ew2,
    mw1,
    mw2,
    own,
    halo,
    part,
    pre,
    cols,
    live,
    fresh,
    gout,
    mout,
    pout,
    pin,
    acc,
    send,
    recv,
    mpre,
    in_sem,
    out_sem,
    own_sems,
    halo_send,
    halo_recv,
    fwd_send,
    fwd_recv,
    swap_send,
    swap_recv,
    msg_send,
    msg_recv,
):
    band = lax.axis_index("lat")
    col = lax.axis_index("lon")
    peer = 1 - col
    width = mesh.shape[1]
    mesh_rows = mesh.shape[0]
    grid_rows = grid.shape[0]
    slots_n = edge.shape[0]
    tiles = slots_n // TILE
    piece = mesh_rows // CHUNKS

    order = [
        (mesh_hbm, mesh),
        (wem_hbm, wem),
        (grid_hbm, grid),
        (weg_hbm, weg),
        (edge_hbm, edge),
        (wee_hbm, wee),
        (ew2_hbm, ew2),
        (gw1_hbm, gw1),
        (gw2_hbm, gw2),
        (mw1_hbm, mw1),
        (mw2_hbm, mw2),
    ]
    loads = [
        pltpu.make_async_copy(a, b, in_sem.at[i]) for i, (a, b) in enumerate(order)
    ]
    for load in loads[:2]:
        load.start()

    has = [band > 0, band < lat_n - 1]
    toward = [band - 1, band + 1]
    barrier = pltpu.get_barrier_semaphore()
    pl.semaphore_signal(barrier, inc=1, device_id={"lon": peer}, device_id_type=MESH)
    for side in range(2):

        @pl.when(has[side])
        def _():
            pl.semaphore_signal(
                barrier, inc=1, device_id={"lat": toward[side]}, device_id_type=MESH
            )

        @pl.when(jnp.logical_not(has[side]))
        def _():
            halo[side] = jnp.zeros((2, mesh_rows, width), jnp.bfloat16)

    loads[0].wait()
    loads[1].wait()
    for load in loads[2:]:
        load.start()
    own[col] = dot(mesh[...], wem[...]).astype(jnp.bfloat16)

    peers = 1 + jnp.minimum(band, 1) + jnp.minimum(lat_n - 1 - band, 1)
    pl.semaphore_wait(barrier, peers)

    def halo_copy(q, side):
        return pltpu.make_async_remote_copy(
            src_ref=own.at[col, pl.ds(q * piece, piece)],
            dst_ref=halo.at[1 - side, col, pl.ds(q * piece, piece)],
            send_sem=halo_send.at[q, side],
            recv_sem=halo_recv.at[q, 1 - side],
            device_id={"lat": toward[side]},
            device_id_type=MESH,
        )

    def halo_arrival(q, side):
        return pltpu.make_async_remote_copy(
            src_ref=own.at[col, pl.ds(q * piece, piece)],
            dst_ref=halo.at[side, col, pl.ds(q * piece, piece)],
            send_sem=halo_send.at[q, side],
            recv_sem=halo_recv.at[q, side],
            device_id={"lat": toward[side]},
            device_id_type=MESH,
        )

    def fwd_copy(q, side):
        return pltpu.make_async_remote_copy(
            src_ref=halo.at[side, col, pl.ds(q * piece, piece)],
            dst_ref=halo.at[side, col, pl.ds(q * piece, piece)],
            send_sem=fwd_send.at[q, side],
            recv_sem=fwd_recv.at[q, side],
            device_id={"lon": peer},
            device_id_type=MESH,
        )

    def fwd_arrival(q, side):
        return pltpu.make_async_remote_copy(
            src_ref=halo.at[side, col, pl.ds(q * piece, piece)],
            dst_ref=halo.at[side, peer, pl.ds(q * piece, piece)],
            send_sem=fwd_send.at[q, side],
            recv_sem=fwd_recv.at[q, side],
            device_id={"lon": peer},
            device_id_type=MESH,
        )

    def send_halo(side):
        @pl.when(has[side])
        def _():
            for q in range(CHUNKS):
                halo_copy(q, side).start()

    send_halo(1)
    own_copy = pltpu.make_async_remote_copy(
        src_ref=own.at[col],
        dst_ref=own.at[col],
        send_sem=own_sems.at[0],
        recv_sem=own_sems.at[1],
        device_id={"lon": peer},
        device_id_type=MESH,
    )
    own_copy.start()

    loads[2].wait()
    loads[3].wait()

    def grid_part(t, carry):
        rows = rows_of(t)
        part[rows, :] = dot(grid[rows, :], weg[...]).astype(jnp.bfloat16)
        return carry

    lax.fori_loop(0, grid_rows // TILE, grid_part, 0)

    loads[4].wait()
    loads[5].wait()
    pltpu.make_async_remote_copy(
        src_ref=own.at[col],
        dst_ref=own.at[peer],
        send_sem=own_sems.at[0],
        recv_sem=own_sems.at[1],
        device_id={"lon": peer},
        device_id_type=MESH,
    ).wait_recv()
    first_grid = (band * 2 + col) * grid_rows
    first_mesh = (band - 1) * 2 * mesh_rows
    live[...] = jnp.where(mask_ref[...] == 1, dst_ref[...] - first_mesh, -1)

    def before_halo(pair, carry):
        for t in (2 * pair, 2 * pair + 1):
            rows = rows_of(t)
            source = spread(src_ref, t)
            target = spread(dst_ref, t) - first_mesh
            cols[rows, :] = target
            total = dot(edge[rows, :], wee[...])
            total += dot(picks(source, [first_grid], grid_rows), part[...])
            total += dot(
                picks(target, [2 * mesh_rows], 2 * mesh_rows),
                own[...].reshape(2 * mesh_rows, width),
            )
            pre[rows, :] = total
        return carry

    lax.fori_loop(0, tiles // 2, before_halo, 0)

    send_halo(0)
    loads[6].wait()

    def forward_halo(side, chunks):
        @pl.when(has[side])
        def _():
            for q in chunks:
                halo_arrival(q, side).wait_recv()
                fwd_copy(q, side).start()

    def receive_halo(side):
        @pl.when(has[side])
        def _():
            for q in range(CHUNKS):
                fwd_arrival(q, side).wait_recv()

    def edge_mlp(side):
        def step(t, carry):
            for k in range(2):
                rows = rows_of(2 * t + k)
                hits = picks(cols[rows, :], [4 * side * mesh_rows], 2 * mesh_rows)
                total = pre[rows, :] + dot(hits, halo[side].reshape(2 * mesh_rows, width))
                mid = silu(total).astype(jnp.bfloat16)
                normed = layer_norm(dot(mid, ew2[...]))
                fresh[rows, :] = (edge[rows, :].astype(jnp.float32) + normed).astype(
                    jnp.bfloat16
                )
            return carry

        lax.fori_loop(0, tiles // 2, step, 0)

    def sums(first):
        ids = lax.broadcasted_iota(jnp.int32, (mesh_rows, 128), 0) + first
        parts = []
        for k in range(slots_n // 128):
            hit = jnp.broadcast_to(live[k : k + 1, :], (mesh_rows, 128)) == ids
            parts.append(jnp.where(hit, 1.0, 0.0).astype(jnp.bfloat16))
        return dot(jnp.concatenate(parts, axis=1), fresh[...])

    def swap(i):
        return pltpu.make_async_remote_copy(
            src_ref=pout.at[i],
            dst_ref=pin.at[i],
            send_sem=swap_send.at[i],
            recv_sem=swap_recv.at[i],
            device_id={"lon": peer},
            device_id_type=MESH,
        )

    some = mesh_rows // PARTS

    def message(side, h):
        return pltpu.make_async_remote_copy(
            src_ref=send.at[side, pl.ds(h * some, some)],
            dst_ref=recv.at[side, pl.ds(h * some, some)],
            send_sem=msg_send.at[side, h],
            recv_sem=msg_recv.at[side, h],
            device_id={"lat": toward[side]},
            device_id_type=MESH,
        )

    def block_first(block, c):
        return (block * 2 + c) * mesh_rows

    def send_message(side):
        @pl.when(has[side])
        def _():
            for h in range(PARTS):
                message(side, h).start()

    forward_halo(0, range(CHUNKS))
    receive_halo(0)
    edge_mlp(0)
    forward_halo(1, range(EARLY))
    pout[0] = sums(block_first(0, peer))
    swap(0).start()
    acc[...] = sums(block_first(0, col))
    swap(0).wait_recv()
    send[0] = (acc[...] + pin[0]).astype(jnp.bfloat16)
    send_message(0)

    forward_halo(1, range(EARLY, CHUNKS))
    pout[2] = sums(block_first(1, peer))
    swap(2).start()
    acc[...] = sums(block_first(1, col))
    receive_halo(1)
    edge_mlp(1)
    pout[1] = sums(block_first(2, peer))
    swap(1).start()
    mpre[...] = sums(block_first(2, col))
    swap(1).wait_recv()
    send[1] = (mpre[...] + pin[1]).astype(jnp.bfloat16)
    send_message(1)

    for i in (7, 8, 9, 10):
        loads[i].wait()

    def grid_mlp(t, carry):
        rows = rows_of(t)
        mid = silu(dot(grid[rows, :], gw1[...])).astype(jnp.bfloat16)
        normed = layer_norm(dot(mid, gw2[...]))
        gout[rows, :] = (grid[rows, :].astype(jnp.float32) + normed).astype(jnp.bfloat16)
        return carry

    lax.fori_loop(0, grid_rows // TILE, grid_mlp, 0)
    store_grid = pltpu.make_async_copy(gout, grid_out, out_sem.at[0])
    store_grid.start()

    mpre[...] = dot(mesh[...], mw1[:width, :])
    swap(2).wait_recv()
    acc[...] += pin[2]
    stores = []
    for h in range(PARTS):
        rows = pl.ds(h * some, some)
        for side in range(2):

            @pl.when(has[1 - side])
            def _():
                message(side, h).wait_recv()
                acc[rows, :] += recv[side, rows, :].astype(jnp.float32)

        mid = silu(
            mpre[rows, :] + dot(acc[rows, :].astype(jnp.bfloat16), mw1[width:, :])
        ).astype(jnp.bfloat16)
        normed = layer_norm(dot(mid, mw2[...]))
        mout[rows, :] = (mesh[rows, :].astype(jnp.float32) + normed).astype(jnp.bfloat16)
        store = pltpu.make_async_copy(
            mout.at[rows], mesh_out.at[rows], out_sem.at[1 + h]
        )
        store.start()
        stores.append(store)

    own_copy.wait_send()
    for i in range(3):
        swap(i).wait_send()
    for side in range(2):

        @pl.when(has[side])
        def _():
            for h in range(PARTS):
                message(side, h).wait_send()
            for q in range(CHUNKS):
                halo_copy(q, side).wait_send()
                fwd_copy(q, side).wait_send()

    store_grid.wait()
    for store in stores:
        store.wait()


def per_device(lat_n, *args):
    (grid_lat, mesh_lat, edge_lat, edge_src, edge_dst, edge_mask) = args[:6]
    weights = args[6:]
    width = mesh_lat.shape[1]
    mesh_rows = mesh_lat.shape[0]
    grid_rows = grid_lat.shape[0]
    slots = edge_lat.shape[0]
    bf16, f32 = jnp.bfloat16, jnp.float32
    dma = pltpu.SemaphoreType.DMA
    vmem = pltpu.VMEM
    scratch = [
        vmem(grid_lat.shape, bf16),
        vmem(mesh_lat.shape, bf16),
        vmem(edge_lat.shape, bf16),
        *[vmem(w.shape, bf16) for w in weights],
        vmem((2, mesh_rows, width), bf16),
        vmem((2, 2, mesh_rows, width), bf16),
        vmem((grid_rows, width), bf16),
        vmem((slots, width), f32),
        vmem((slots, 128), jnp.int32),
        vmem((slots // 128, 128), jnp.int32),
        vmem((slots, width), bf16),
        vmem((grid_rows, width), bf16),
        vmem((mesh_rows, width), bf16),
        vmem((3, mesh_rows, width), f32),
        vmem((3, mesh_rows, width), f32),
        vmem((mesh_rows, width), f32),
        vmem((2, mesh_rows, width), bf16),
        vmem((2, mesh_rows, width), bf16),
        vmem((mesh_rows, width), f32),
        dma((11,)),
        dma((1 + PARTS,)),
        dma((2,)),
        dma((CHUNKS, 2)),
        dma((CHUNKS, 2)),
        dma((CHUNKS, 2)),
        dma((CHUNKS, 2)),
        dma((3,)),
        dma((3,)),
        dma((2, PARTS)),
        dma((2, PARTS)),
    ]
    in_vmem = pl.BlockSpec(memory_space=pltpu.VMEM)
    anywhere = pl.BlockSpec(memory_space=pl.ANY)
    return pl.pallas_call(
        functools.partial(kernel, lat_n),
        out_shape=(
            jax.ShapeDtypeStruct(mesh_lat.shape, bf16),
            jax.ShapeDtypeStruct(grid_lat.shape, bf16),
        ),
        in_specs=[in_vmem] * 3 + [anywhere] * 11,
        out_specs=(anywhere, anywhere),
        scratch_shapes=scratch,
        compiler_params=pltpu.CompilerParams(
            collective_id=0, has_side_effects=True, vmem_limit_bytes=VMEM_BYTES
        ),
    )(
        *[a.reshape(slots // 128, 128) for a in (edge_src, edge_dst, edge_mask)],
        grid_lat,
        mesh_lat,
        edge_lat,
        *weights,
    )


def solution(mesh):
    rows = P(("groups", "lat", "lon"), None)
    line = P(("groups", "lat", "lon"))
    return jax.shard_map(
        functools.partial(per_device, mesh.shape["lat"]),
        mesh=mesh,
        in_specs=(rows,) * 3 + (line,) * 3 + (P(),) * 8,
        out_specs=(rows, rows),
        check_vma=False,
    )
```

```python
import functools

import jax
import jax.numpy as jnp
from jax import lax
from jax.experimental import pallas as pl
from jax.experimental.pallas import tpu as pltpu
from jax.sharding import PartitionSpec as P

TILE = 256
CHUNKS = 2
VMEM_BYTES = 63 * 2**20
MESH = pl.DeviceIdType.MESH


def silu(v):
    half = 0.5 * v
    return half + half * jnp.tanh(half)


def layer_norm(values):
    mean = jnp.mean(values, axis=-1, keepdims=True)
    centered = values - mean
    variance = jnp.mean(centered * centered, axis=-1, keepdims=True)
    return centered * lax.rsqrt(variance + 1e-05)


def dot(a, b):
    return jnp.dot(a, b, preferred_element_type=jnp.float32)


def spread(ref, tile):
    parts = []
    for k in range(TILE // 128):
        row = ref[pl.ds(tile * (TILE // 128) + k, 1), :]
        parts.append(jnp.broadcast_to(row, (128, 128)).T)
    return jnp.concatenate(parts, axis=0)


def picks(cols, bases, width):
    lanes = lax.broadcasted_iota(jnp.int32, (TILE, 128), 1)
    parts = []
    for base in bases:
        for k in range(width // 128):
            hit = cols == lanes + (base + 128 * k)
            parts.append(jnp.where(hit, 1.0, 0.0).astype(jnp.bfloat16))
    return jnp.concatenate(parts, axis=1)


def rows_of(tile):
    return pl.ds(pl.multiple_of(tile * TILE, TILE), TILE)


def kernel(
    lat_n,
    src_ref,
    dst_ref,
    mask_ref,
    grid_hbm,
    mesh_hbm,
    edge_hbm,
    gw1_hbm,
    gw2_hbm,
    wee_hbm,
    weg_hbm,
    wem_hbm,
    ew2_hbm,
    mw1_hbm,
    mw2_hbm,
    mesh_out,
    grid_out,
    grid,
    mesh,
    edge,
    gw1,
    gw2,
    wee,
    weg,
    wem,
    ew2,
    mw1,
    mw2,
    own,
    halo,
    part,
    pre,
    cols,
    live,
    fresh,
    gout,
    mout,
    pout,
    pin,
    acc,
    send,
    recv,
    mpre,
    in_sem,
    out_sem,
    own_sems,
    halo_send,
    halo_recv,
    fwd_send,
    fwd_recv,
    swap_send,
    swap_recv,
    msg_send,
    msg_recv,
):
    band = lax.axis_index("lat")
    col = lax.axis_index("lon")
    peer = 1 - col
    width = mesh.shape[1]
    mesh_rows = mesh.shape[0]
    grid_rows = grid.shape[0]
    slots_n = edge.shape[0]
    tiles = slots_n // TILE
    piece = mesh_rows // CHUNKS

    order = [
        (mesh_hbm, mesh),
        (wem_hbm, wem),
        (grid_hbm, grid),
        (weg_hbm, weg),
        (edge_hbm, edge),
        (wee_hbm, wee),
        (ew2_hbm, ew2),
        (gw1_hbm, gw1),
        (gw2_hbm, gw2),
        (mw1_hbm, mw1),
        (mw2_hbm, mw2),
    ]
    loads = [
        pltpu.make_async_copy(a, b, in_sem.at[i]) for i, (a, b) in enumerate(order)
    ]
    for load in loads[:2]:
        load.start()

    has = [band > 0, band < lat_n - 1]
    toward = [band - 1, band + 1]
    barrier = pltpu.get_barrier_semaphore()
    pl.semaphore_signal(barrier, inc=1, device_id={"lon": peer}, device_id_type=MESH)
    for side in range(2):

        @pl.when(has[side])
        def _():
            pl.semaphore_signal(
                barrier, inc=1, device_id={"lat": toward[side]}, device_id_type=MESH
            )

        @pl.when(jnp.logical_not(has[side]))
        def _():
            halo[side] = jnp.zeros((2, mesh_rows, width), jnp.bfloat16)

    loads[0].wait()
    loads[1].wait()
    for load in loads[2:]:
        load.start()
    own[col] = dot(mesh[...], wem[...]).astype(jnp.bfloat16)

    peers = 1 + jnp.minimum(band, 1) + jnp.minimum(lat_n - 1 - band, 1)
    pl.semaphore_wait(barrier, peers)

    def halo_copy(q, side):
        return pltpu.make_async_remote_copy(
            src_ref=own.at[col, pl.ds(q * piece, piece)],
            dst_ref=halo.at[1 - side, col, pl.ds(q * piece, piece)],
            send_sem=halo_send.at[q, side],
            recv_sem=halo_recv.at[q, 1 - side],
            device_id={"lat": toward[side]},
            device_id_type=MESH,
        )

    def halo_arrival(q, side):
        return pltpu.make_async_remote_copy(
            src_ref=own.at[col, pl.ds(q * piece, piece)],
            dst_ref=halo.at[side, col, pl.ds(q * piece, piece)],
            send_sem=halo_send.at[q, side],
            recv_sem=halo_recv.at[q, side],
            device_id={"lat": toward[side]},
            device_id_type=MESH,
        )

    def fwd_copy(q, side):
        return pltpu.make_async_remote_copy(
            src_ref=halo.at[side, col, pl.ds(q * piece, piece)],
            dst_ref=halo.at[side, col, pl.ds(q * piece, piece)],
            send_sem=fwd_send.at[q, side],
            recv_sem=fwd_recv.at[q, side],
            device_id={"lon": peer},
            device_id_type=MESH,
        )

    def fwd_arrival(q, side):
        return pltpu.make_async_remote_copy(
            src_ref=halo.at[side, col, pl.ds(q * piece, piece)],
            dst_ref=halo.at[side, peer, pl.ds(q * piece, piece)],
            send_sem=fwd_send.at[q, side],
            recv_sem=fwd_recv.at[q, side],
            device_id={"lon": peer},
            device_id_type=MESH,
        )

    def send_halo(side):
        @pl.when(has[side])
        def _():
            for q in range(CHUNKS):
                halo_copy(q, side).start()

    send_halo(1)
    own_copy = pltpu.make_async_remote_copy(
        src_ref=own.at[col],
        dst_ref=own.at[col],
        send_sem=own_sems.at[0],
        recv_sem=own_sems.at[1],
        device_id={"lon": peer},
        device_id_type=MESH,
    )
    own_copy.start()

    loads[2].wait()
    loads[3].wait()

    def grid_part(t, carry):
        rows = rows_of(t)
        part[rows, :] = dot(grid[rows, :], weg[...]).astype(jnp.bfloat16)
        return carry

    lax.fori_loop(0, grid_rows // TILE, grid_part, 0)

    loads[4].wait()
    loads[5].wait()
    pltpu.make_async_remote_copy(
        src_ref=own.at[col],
        dst_ref=own.at[peer],
        send_sem=own_sems.at[0],
        recv_sem=own_sems.at[1],
        device_id={"lon": peer},
        device_id_type=MESH,
    ).wait_recv()
    first_grid = (band * 2 + col) * grid_rows
    first_mesh = (band - 1) * 2 * mesh_rows
    live[...] = jnp.where(mask_ref[...] == 1, dst_ref[...] - first_mesh, -1)

    def before_halo(t, carry):
        rows = rows_of(t)
        source = spread(src_ref, t)
        target = spread(dst_ref, t) - first_mesh
        cols[rows, :] = target
        total = dot(edge[rows, :], wee[...])
        total += dot(picks(source, [first_grid], grid_rows), part[...])
        total += dot(
            picks(target, [2 * mesh_rows], 2 * mesh_rows),
            own[...].reshape(2 * mesh_rows, width),
        )
        pre[rows, :] = total
        return carry

    lax.fori_loop(0, tiles, before_halo, 0)

    send_halo(0)
    loads[6].wait()

    def receive_halo(side):
        @pl.when(has[side])
        def _():
            for q in range(CHUNKS):
                halo_arrival(q, side).wait_recv()
                fwd_copy(q, side).start()
            for q in range(CHUNKS):
                fwd_arrival(q, side).wait_recv()

    def edge_mlp(side):
        def step(t, carry):
            for k in range(2):
                rows = rows_of(2 * t + k)
                hits = picks(cols[rows, :], [4 * side * mesh_rows], 2 * mesh_rows)
                total = pre[rows, :] + dot(hits, halo[side].reshape(2 * mesh_rows, width))
                mid = silu(total).astype(jnp.bfloat16)
                normed = layer_norm(dot(mid, ew2[...]))
                fresh[rows, :] = (edge[rows, :].astype(jnp.float32) + normed).astype(
                    jnp.bfloat16
                )
            return carry

        lax.fori_loop(0, tiles // 2, step, 0)

    def sums(first):
        ids = lax.broadcasted_iota(jnp.int32, (mesh_rows, 128), 0) + first
        parts = []
        for k in range(slots_n // 128):
            hit = jnp.broadcast_to(live[k : k + 1, :], (mesh_rows, 128)) == ids
            parts.append(jnp.where(hit, 1.0, 0.0).astype(jnp.bfloat16))
        return dot(jnp.concatenate(parts, axis=1), fresh[...])

    def swap(i):
        return pltpu.make_async_remote_copy(
            src_ref=pout.at[i],
            dst_ref=pin.at[i],
            send_sem=swap_send.at[i],
            recv_sem=swap_recv.at[i],
            device_id={"lon": peer},
            device_id_type=MESH,
        )

    def message(side):
        return pltpu.make_async_remote_copy(
            src_ref=send.at[side],
            dst_ref=recv.at[side],
            send_sem=msg_send.at[side],
            recv_sem=msg_recv.at[side],
            device_id={"lat": toward[side]},
            device_id_type=MESH,
        )

    def block_first(block, c):
        return (block * 2 + c) * mesh_rows

    for side in range(2):
        receive_halo(side)
        edge_mlp(side)
        pout[side] = sums(block_first(2 * side, peer)).astype(jnp.bfloat16)
        swap(side).start()
        acc[...] = sums(block_first(2 * side, col))
        swap(side).wait_recv()
        send[side] = (acc[...] + pin[side].astype(jnp.float32)).astype(jnp.bfloat16)

        @pl.when(has[side])
        def _():
            message(side).start()

    pout[2] = sums(block_first(1, peer)).astype(jnp.bfloat16)
    swap(2).start()
    acc[...] = sums(block_first(1, col))

    for i in (7, 8, 9, 10):
        loads[i].wait()

    def grid_mlp(t, carry):
        rows = rows_of(t)
        mid = silu(dot(grid[rows, :], gw1[...])).astype(jnp.bfloat16)
        normed = layer_norm(dot(mid, gw2[...]))
        gout[rows, :] = (grid[rows, :].astype(jnp.float32) + normed).astype(jnp.bfloat16)
        return carry

    lax.fori_loop(0, grid_rows // TILE, grid_mlp, 0)
    store_grid = pltpu.make_async_copy(gout, grid_out, out_sem.at[0])
    store_grid.start()

    mpre[...] = dot(mesh[...], mw1[:width, :])
    swap(2).wait_recv()
    acc[...] += pin[2].astype(jnp.float32)
    for side in range(2):

        @pl.when(has[1 - side])
        def _():
            message(side).wait_recv()
            acc[...] += recv[side].astype(jnp.float32)

    mid = silu(mpre[...] + dot(acc[...].astype(jnp.bfloat16), mw1[width:, :])).astype(
        jnp.bfloat16
    )
    normed = layer_norm(dot(mid, mw2[...]))
    mout[...] = (mesh[...].astype(jnp.float32) + normed).astype(jnp.bfloat16)
    store_mesh = pltpu.make_async_copy(mout, mesh_out, out_sem.at[1])
    store_mesh.start()

    own_copy.wait_send()
    for i in range(3):
        swap(i).wait_send()
    for side in range(2):

        @pl.when(has[side])
        def _():
            message(side).wait_send()
            for q in range(CHUNKS):
                halo_copy(q, side).wait_send()
                fwd_copy(q, side).wait_send()

    store_grid.wait()
    store_mesh.wait()


def per_device(lat_n, *args):
    (grid_lat, mesh_lat, edge_lat, edge_src, edge_dst, edge_mask) = args[:6]
    weights = args[6:]
    width = mesh_lat.shape[1]
    mesh_rows = mesh_lat.shape[0]
    grid_rows = grid_lat.shape[0]
    slots = edge_lat.shape[0]
    bf16, f32 = jnp.bfloat16, jnp.float32
    dma = pltpu.SemaphoreType.DMA
    vmem = pltpu.VMEM
    scratch = [
        vmem(grid_lat.shape, bf16),
        vmem(mesh_lat.shape, bf16),
        vmem(edge_lat.shape, bf16),
        *[vmem(w.shape, bf16) for w in weights],
        vmem((2, mesh_rows, width), bf16),
        vmem((2, 2, mesh_rows, width), bf16),
        vmem((grid_rows, width), bf16),
        vmem((slots, width), f32),
        vmem((slots, 128), jnp.int32),
        vmem((slots // 128, 128), jnp.int32),
        vmem((slots, width), bf16),
        vmem((grid_rows, width), bf16),
        vmem((mesh_rows, width), bf16),
        vmem((3, mesh_rows, width), bf16),
        vmem((3, mesh_rows, width), bf16),
        vmem((mesh_rows, width), f32),
        vmem((2, mesh_rows, width), bf16),
        vmem((2, mesh_rows, width), bf16),
        vmem((mesh_rows, width), f32),
        dma((11,)),
        dma((2,)),
        dma((2,)),
        dma((CHUNKS, 2)),
        dma((CHUNKS, 2)),
        dma((CHUNKS, 2)),
        dma((CHUNKS, 2)),
        dma((3,)),
        dma((3,)),
        dma((2,)),
        dma((2,)),
    ]
    in_vmem = pl.BlockSpec(memory_space=pltpu.VMEM)
    anywhere = pl.BlockSpec(memory_space=pl.ANY)
    return pl.pallas_call(
        functools.partial(kernel, lat_n),
        out_shape=(
            jax.ShapeDtypeStruct(mesh_lat.shape, bf16),
            jax.ShapeDtypeStruct(grid_lat.shape, bf16),
        ),
        in_specs=[in_vmem] * 3 + [anywhere] * 11,
        out_specs=(anywhere, anywhere),
        scratch_shapes=scratch,
        compiler_params=pltpu.CompilerParams(
            collective_id=0, has_side_effects=True, vmem_limit_bytes=VMEM_BYTES
        ),
    )(
        *[a.reshape(slots // 128, 128) for a in (edge_src, edge_dst, edge_mask)],
        grid_lat,
        mesh_lat,
        edge_lat,
        *weights,
    )


def solution(mesh):
    rows = P(("groups", "lat", "lon"), None)
    line = P(("groups", "lat", "lon"))
    return jax.shard_map(
        functools.partial(per_device, mesh.shape["lat"]),
        mesh=mesh,
        in_specs=(rows,) * 3 + (line,) * 3 + (P(),) * 8,
        out_specs=(rows, rows),
        check_vma=False,
    )
```
